32 devices in a mesh: runs: 8 (over z, x), chan: 4 (over y, core).
Axes of the slice: x: 2, y: 2, z: 4, core: 2. Of those that a mesh axis runs over, the one named last changes fastest.
Arguments:
- slices: bfloat16 [64, 512, 8192], P('runs', None, 'chan'), may hold values from -6 to 6
- spectra: bfloat16 [2, 48, 8192], P(None, None, 'chan'), may hold values from -0.0625 to 0.0625
- loadings: float32 [64, 48], replicated, may hold values from 0.5 to 2
- mixing: float32 [2, 48, 48], replicated, may hold values from -1 to 3.5
- halves: int32 [64], replicated, may hold values from 0 to 1, as said below
- partner: int32 [64], replicated, may hold values from 0 to 63, as said below
Outputs:
- new_spectra: float32 [2, 48, 8192], P(None, None, 'chan')
- held_residual: float32 [64, 48, 8192], P('runs', None, 'chan')
The draws below stay inside these ranges and needn't reach their ends.
Inputs may be any that keep to these rules, and one draw needn't show every extreme that they name: `halves`: exactly half of the 64 runs are in each half. partner pairs every run with a run of the other half, and the partner of a run's partner is the run itself.
All inputs are finite; a program needn't handle non-finite values.
Results may differ from the reference program's by a relative error of at most 0.0045.
Values may be sent and summed in bfloat16 or wider, within the bound.
A program may use at most 64 MiB of HBM per device.

```python
import math
import jax
import jax.numpy as jnp
from jax import lax

R = 48
TIMES = 512
J = 8192
NS_STEPS = 10
RUNS = 64


def pairing(key):
    order = jax.random.permutation(jax.random.fold_in(key, 11), RUNS).astype(jnp.int32)
    middle = RUNS // 2
    places = jnp.arange(RUNS, dtype=jnp.int32)
    labels = jnp.zeros((RUNS,), jnp.int32).at[order].set((places >= middle).astype(jnp.int32))
    mates = jnp.zeros((RUNS,), jnp.int32).at[order].set(jnp.roll(order, middle))
    return (labels, mates)


def draw_halves(key, part):
    return pairing(key)[0]


def draw_partner(key, part):
    return pairing(key)[1]


def draw_slices(key, part):
    first = jax.random.fold_in(jax.random.fold_in(key, 7), 0)
    values = jnp.clip(jax.random.normal(first, (RUNS, TIMES, J), jnp.float32), -6.0, 6.0)
    return values.astype(jnp.bfloat16)


def draw_mixing(key, part):
    first, second = jax.random.split(jax.random.fold_in(key, 5))
    diagonal = jax.random.uniform(first, (2, R), jnp.float32, 2.0, 3.0)
    spread = jnp.clip(0.12 * jax.random.normal(second, (2, R, R), jnp.float32), -0.45, 0.45)
    return spread + diagonal[:, :, None] * jnp.eye(R, dtype=jnp.float32)[None]


def shard_levels(own_key, dims, pieces, smallest, high):
    gain = 1.0
    for dim, shards_of in pieces:
        draws = jax.random.uniform(jax.random.fold_in(jax.random.fold_in(own_key, 6), dim), (shards_of,), jnp.float32, smallest / len(pieces), high / len(pieces))
        gain = gain * jnp.repeat(jnp.exp(draws), dims[dim] // shards_of).reshape((-1,) + (1,) * (len(dims) - 1 - dim))
    return gain


def noise(rng, dims, width, bound, cuts=(), held_as=jnp.bfloat16):
    result = jax.random.normal(rng, dims, jnp.float32) * width
    if len(cuts) > 0:
        result = shard_levels(rng, dims, cuts, -0.22, 0.18) * result
    return jnp.clip(result, min=-bound, max=bound).astype(held_as)


def setup_inputs(seed: int = 0) -> dict:
    key_list = jax.random.split(jax.random.key(seed), 7)
    slices = draw_slices(jax.random.fold_in(key_list[6], 71), 0)
    spectra = noise(key_list[1], (2, R, J), J ** -0.5, 0.0625, ((2, 4),))
    loadings = jnp.clip(jnp.exp(jax.random.uniform(key_list[2], (RUNS, R), jnp.float32, math.log(0.5), math.log(2.0))), 0.5, 2.0)
    mixing = draw_mixing(jax.random.fold_in(key_list[6], 71), 0)
    halves = draw_halves(jax.random.fold_in(key_list[6], 71), 0)
    partner = draw_partner(jax.random.fold_in(key_list[6], 71), 0)
    return dict(slices=slices, spectra=spectra, loadings=loadings, mixing=mixing, halves=halves, partner=partner)


def polar_scale(gram):
    eye_rank = jnp.eye(gram.shape[-1], dtype=gram.dtype)
    start = eye_rank / jnp.sqrt(jnp.trace(gram) + 1e-06)

    def advance(step, factor):
        inner = jnp.dot(jnp.dot(factor.T, gram, precision=lax.Precision.HIGHEST), factor, precision=lax.Precision.HIGHEST)
        return 0.5 * jnp.dot(factor, 3.0 * eye_rank - inner, precision=lax.Precision.HIGHEST)
    return lax.fori_loop(0, NS_STEPS, advance, start)

def project(slice_run, rows_low, mixed):
    basis = jnp.dot(rows_low.astype(jnp.float32), slice_run.T.astype(jnp.float32), preferred_element_type=jnp.float32)
    scaled = jnp.dot(mixed, basis, precision=lax.Precision.HIGHEST)
    gram = jnp.dot(scaled, scaled.T, precision=lax.Precision.HIGHEST)
    factor = polar_scale(gram)
    rotated = jnp.dot(factor.T, scaled, precision=lax.Precision.HIGHEST).astype(jnp.bfloat16)
    return jnp.dot(rotated.astype(jnp.float32), slice_run.astype(jnp.float32), preferred_element_type=jnp.float32)

def solve_one(lower, target):
    return jax.scipy.linalg.cho_solve((lower, True), target)

def reference(slices, spectra, loadings, mixing, halves, partner):

    def fit_step(total, item):
        slice_run, half_id, loading = item
        mixed = mixing[half_id] * loading[None, :]
        projected = project(slice_run, spectra[half_id], mixed)
        term = jnp.dot(mixed.T, projected, precision=lax.Precision.HIGHEST)
        member_one = (jnp.arange(2, dtype=jnp.int32) == half_id).astype(total.dtype)
        return (total + member_one[:, None, None] * term[None], None)
    empty = jnp.zeros((2, R, J), jnp.float32)
    moments, _ = lax.scan(fit_step, empty, (slices, halves, loadings))
    member = (halves[:, None] == jnp.arange(2, dtype=jnp.int32)[None, :]).astype(loadings.dtype)
    cross = jnp.einsum('kh,kr,ks->hrs', member, loadings, loadings, precision=lax.Precision.HIGHEST)
    inner_mix = jnp.einsum('hsr,hst->hrt', mixing, mixing, precision=lax.Precision.HIGHEST)
    system = inner_mix * cross
    lower = jnp.linalg.cholesky(system)
    new_spectra = jax.vmap(solve_one)(lower, moments)

    def held_step(item):
        slice_run, half_id, mate = item
        other = 1 - half_id
        mixed = mixing[other] * loadings[mate][None, :]
        fitted = new_spectra[other]
        projected = project(slice_run, fitted.astype(jnp.bfloat16), mixed)
        return projected - jnp.dot(mixed, fitted, precision=lax.Precision.HIGHEST)
    held_residual = lax.map(held_step, (slices, halves, partner))
    return (new_spectra, held_residual)
```

```python
import functools

import jax
import jax.numpy as jnp
from jax import lax
from jax.experimental import pallas as pl
from jax.experimental.pallas import tpu as pltpu
from jax.sharding import PartitionSpec as P

NS_STEPS = 10
HI = lax.Precision.HIGHEST
F32 = jnp.float32
BF16 = jnp.bfloat16
NT = (((1,), (1,)), ((), ()))
MESH = pl.DeviceIdType.MESH


def mul(a, b):
    return jnp.dot(a, b, precision=HI, preferred_element_type=F32)


def identity(size):
    rows = lax.broadcasted_iota(jnp.int32, (size, size), 0)
    cols = lax.broadcasted_iota(jnp.int32, (size, size), 1)
    return (rows == cols).astype(F32)


def polar_rotate(mixes, bases):
    rank = mixes[0].shape[0]
    eye = identity(rank)
    scaled = [mul(m, b) for m, b in zip(mixes, bases)]
    grams = [lax.dot_general(s, s, NT, precision=HI, preferred_element_type=F32) for s in scaled]
    traces = [jnp.sum(jnp.sum(g * eye, axis=1, keepdims=True), axis=0, keepdims=True) + 1e-06 for g in grams]
    ys = [g / t for g, t in zip(grams, traces)]
    xs = [eye * lax.rsqrt(t) for t in traces]
    for step in range(NS_STEPS):
        zs = [1.5 * eye - 0.5 * y for y in ys]
        if step == 0:
            xs = [z * lax.rsqrt(t) for z, t in zip(zs, traces)]
        else:
            xs = [mul(x, z) for x, z in zip(xs, zs)]
        if step < NS_STEPS - 1:
            ws = [mul(y, z) for y, z in zip(ys, zs)]
            ys = [mul(w, z) for w, z in zip(ws, zs)]
    return [mul(x, s) for x, s in zip(xs, scaled)]


def invert_pair(systems):
    rank = systems[0].shape[0]
    eye = identity(rank)
    lane = lax.broadcasted_iota(jnp.int32, (rank, 2 * rank), 1)
    sub = lax.broadcasted_iota(jnp.int32, (rank, 2 * rank), 0)

    def step(j, tables):
        out = []
        for t in tables:
            col = jnp.sum(jnp.where(lane == j, t, 0.0), axis=1, keepdims=True)
            row = jnp.sum(jnp.where(sub == j, t, 0.0), axis=0, keepdims=True)
            pivot = jnp.sum(jnp.where(sub[:, :1] == j, col, 0.0), axis=0, keepdims=True)
            scaled = row / pivot
            out.append(jnp.where(sub == j, scaled, t - col * scaled))
        return out

    tables = [jnp.concatenate([a, eye], axis=1) for a in systems]
    tables = lax.fori_loop(0, rank, step, tables)
    return [t[:, rank:] for t in tables]


def kernel(
    n, sl, sp, omix, hmix, hf, sysm, new_o, res_o,
    s, bs1, br1, own1, gb, psend, p32, rrecv, fitb, rows, gcat, bs2, br2, own2, rot,
    dsem, s1s, s1r, s2s, s2r, s3s, s3r, s4s, s4r, s5s, s5r, s6s, s6r,
):
    c = lax.axis_index("chan")
    r = lax.axis_index("runs")
    count, times, width = sl.shape
    rank = omix.shape[1]
    per = count // 4
    blocks = n // 2
    w = width // blocks
    peers = [(c + 2) % 4, 3 - c, c + 1 - 2 * (c % 2)]
    order = [p * per + i for p in peers + [c] for i in range(per)]

    def rows_of(k):
        return pl.ds(pl.multiple_of(k * times, times), times)

    loads = []
    for t, k in enumerate(order):
        load = pltpu.make_async_copy(sl.at[k], s.at[rows_of(k)], dsem.at[t])
        load.start()
        loads.append(load)

    barrier = pltpu.get_barrier_semaphore()
    for p in peers:
        pl.semaphore_signal(barrier, inc=1, device_id={"chan": p}, device_id_type=MESH)
    for d in range(1, n):
        pl.semaphore_signal(barrier, inc=1, device_id={"runs": (r + d) % n}, device_id_type=MESH)
    pl.semaphore_wait(barrier, 3 + n - 1)

    def remote(src, dst, ssem, rsem, where):
        return pltpu.make_async_remote_copy(
            src_ref=src, dst_ref=dst, send_sem=ssem, recv_sem=rsem, device_id=where, device_id_type=MESH
        )

    def basis_phase(both, flip, bs, br, own, ssem, rsem, waits):
        sends = []
        for t, k in enumerate(order):
            if waits:
                loads[t].wait()
            part = lax.dot_general(s[rows_of(k)], both, NT, preferred_element_type=F32).T
            h = hf[k]
            if flip:
                h = 1.0 - h
            chosen = part[:rank] * (1.0 - h) + part[rank:] * h
            q, i = t // per, t % per
            if q < 3:
                bs[k] = chosen.astype(BF16)
                if i == per - 1:
                    p = peers[q]
                    send = remote(
                        bs.at[pl.ds(p * per, per)], br.at[c], ssem.at[q], rsem.at[c], {"chan": p}
                    )
                    send.start()
                    sends.append(send)
            else:
                own[i] = chosen
        return sends

    def basis_sum(bs, br, own, ssem, rsem):
        for q, p in enumerate(peers):
            remote(
                bs.at[pl.ds(p * per, per)], br.at[p], ssem.at[q], rsem.at[p], {"chan": p}
            ).wait_recv()
        return [
            own[i] + br[peers[0], i].astype(F32) + br[peers[1], i].astype(F32) + br[peers[2], i].astype(F32)
            for i in range(per)
        ]

    def share(buf, ssem, rsem):
        mine = buf.at[pl.ds(c * per, per)]
        sends = []
        for q, p in enumerate(peers):
            send = remote(mine, mine, ssem.at[q], rsem.at[c], {"chan": p})
            send.start()
            sends.append(send)
        return sends

    def shared(buf, ssem, rsem):
        for q, p in enumerate(peers):
            theirs = buf.at[pl.ds(p * per, per)]
            remote(theirs, theirs, ssem.at[q], rsem.at[p], {"chan": p}).wait_recv()

    sends = basis_phase(sp[...], False, bs1, br1, own1, s1s, s1r, True)
    inverses = invert_pair([sysm[0], sysm[1]])
    backs = []
    for i in range(per):
        h = hf[c * per + i]
        chosen = inverses[0] * (1.0 - h) + inverses[1] * h
        backs.append(
            lax.dot_general(chosen, omix[c * per + i], NT, precision=HI, preferred_element_type=F32)
        )
    bases = basis_sum(bs1, br1, own1, s1s, s1r)
    rotated = polar_rotate([omix[c * per + i] for i in range(per)], bases)
    for i in range(per):
        low = rotated[i].astype(BF16).astype(F32)
        gb[c * per + i] = mul(backs[i], low).astype(BF16)
    sends += share(gb, s2s, s2r)
    shared(gb, s2s, s2r)
    for k in range(count):
        h = hf[k]
        g = gb[k].astype(F32)
        gcat[:rank, k * times : (k + 1) * times] = (g * (1.0 - h)).astype(BF16)
        gcat[rank:, k * times : (k + 1) * times] = (g * h).astype(BF16)

    def chunk(block):
        cols = pl.ds(pl.multiple_of(block * w, w), w)
        return jnp.dot(gcat[...], s[:, cols], preferred_element_type=F32)

    def send_chunk(j, d):
        send = remote(psend.at[j], rrecv.at[r], s3s.at[d], s3r.at[r], {"runs": j})
        send.start()
        sends.append(send)

    count_sent = 0
    for step in range(1, blocks):
        block = (r + step) % blocks
        part = chunk(block)
        for half in range(2):
            j = half * blocks + block
            psend[j] = part[half * rank : (half + 1) * rank].astype(BF16)
            send_chunk(j, count_sent)
            count_sent += 1
    part = chunk(r % blocks)
    p32[0] = part[:rank]
    p32[1] = part[rank:]
    j = (r + blocks) % n
    psend[j] = p32[1 - r // blocks].astype(BF16)
    send_chunk(j, count_sent)
    total = p32[r // blocks]
    for d in range(1, n):
        j = (r + d) % n
        remote(psend.at[j], rrecv.at[j], s3s.at[d - 1], s3r.at[j], {"runs": j}).wait_recv()
        total = total + rrecv[j].astype(F32)
    fitb[r] = total.astype(BF16)
    for d in range(1, n):
        send = remote(fitb.at[r], fitb.at[r], s4s.at[d - 1], s4r.at[r], {"runs": (r + d) % n})
        send.start()
        sends.append(send)
    for d in range(1, n):
        j = (r + d) % n
        remote(fitb.at[j], fitb.at[j], s4s.at[d - 1], s4r.at[j], {"runs": j}).wait_recv()
    for half in range(2):
        for block in range(blocks):
            low = fitb[half * blocks + block]
            rows[half * rank : (half + 1) * rank, block * w : (block + 1) * w] = low
            new_o[half, :, block * w : (block + 1) * w] = low.astype(F32)

    sends += basis_phase(rows[...], True, bs2, br2, own2, s5s, s5r, False)

    def model(k):
        h = hf[k]
        m = hmix[k]
        high = m.astype(BF16).astype(F32)
        parts = [high, m - high]
        left = jnp.concatenate(
            [jnp.concatenate([v * h, v * (1.0 - h)], axis=1) for v in parts], axis=0
        ).astype(BF16)
        both = jnp.dot(left, rows[...], preferred_element_type=F32)
        return both[:rank] + both[rank:]

    for k in range(count):
        res_o[k] = model(k)
    bases = basis_sum(bs2, br2, own2, s5s, s5r)
    rotated = polar_rotate([hmix[c * per + i] for i in range(per)], bases)
    for i in range(per):
        rot[c * per + i] = rotated[i].astype(BF16)
    sends += share(rot, s6s, s6r)
    shared(rot, s6s, s6r)
    for k in range(count):
        res_o[k] = (
            jnp.dot(rot[k], s[k * times : (k + 1) * times], preferred_element_type=F32) - res_o[k]
        )
    for send in sends:
        send.wait_send()


def body(n, slices, spectra, loadings, mixing, halves, partner):
    run_count, times, width = slices.shape
    rank = mixing.shape[-1]
    total_runs = loadings.shape[0]
    first_run = lax.axis_index("runs") * run_count
    mine = first_run + jnp.arange(run_count, dtype=jnp.int32)
    all_runs = jnp.arange(total_runs, dtype=jnp.int32)
    matches = all_runs[None, :] == mine[:, None]
    my_halves = jnp.sum(jnp.where(matches, halves[None, :], 0), axis=1)
    my_mates = jnp.sum(jnp.where(matches, partner[None, :], 0), axis=1)
    my_loads = jnp.dot(matches.astype(F32), loadings, precision=HI)
    mate_match = (all_runs[None, :] == my_mates[:, None]).astype(F32)
    mate_loads = jnp.dot(mate_match, loadings, precision=HI)
    first_half = (my_halves == 0)[:, None, None]
    own_mix = jnp.where(first_half, mixing[0][None], mixing[1][None]) * my_loads[:, None, :]
    held_mix = jnp.where(first_half, mixing[1][None], mixing[0][None]) * mate_loads[:, None, :]
    member = (halves[:, None] == jnp.arange(2, dtype=jnp.int32)[None, :]).astype(F32)
    cross = jnp.einsum("kh,kr,ks->hrs", member, loadings, loadings, precision=HI)
    inner_mix = jnp.einsum("hsr,hst->hrt", mixing, mixing, precision=HI)
    system = inner_mix * cross

    per = run_count // 4
    w = 2 * width // n
    vmem = pl.BlockSpec(memory_space=pltpu.VMEM)
    dma = pltpu.SemaphoreType.DMA
    new_spectra, residual = pl.pallas_call(
        functools.partial(kernel, n),
        out_shape=(
            jax.ShapeDtypeStruct((2, rank, width), F32),
            jax.ShapeDtypeStruct((run_count, rank, width), F32),
        ),
        in_specs=[
            pl.BlockSpec(memory_space=pl.ANY), vmem, vmem, vmem,
            pl.BlockSpec(memory_space=pltpu.SMEM), vmem,
        ],
        out_specs=(vmem, vmem),
        scratch_shapes=[
            pltpu.VMEM((run_count * times, width), BF16),
            pltpu.VMEM((run_count, rank, times), BF16),
            pltpu.VMEM((4, per, rank, times), BF16),
            pltpu.VMEM((per, rank, times), F32),
            pltpu.VMEM((run_count, rank, times), BF16),
            pltpu.VMEM((n, rank, w), BF16),
            pltpu.VMEM((2, rank, w), F32),
            pltpu.VMEM((n, rank, w), BF16),
            pltpu.VMEM((n, rank, w), BF16),
            pltpu.VMEM((2 * rank, width), BF16),
            pltpu.VMEM((2 * rank, run_count * times), BF16),
            pltpu.VMEM((run_count, rank, times), BF16),
            pltpu.VMEM((4, per, rank, times), BF16),
            pltpu.VMEM((per, rank, times), F32),
            pltpu.VMEM((run_count, rank, times), BF16),
            dma((run_count,)),
            dma((3,)), dma((4,)),
            dma((3,)), dma((4,)),
            dma((n - 1,)), dma((n,)),
            dma((n - 1,)), dma((n,)),
            dma((3,)), dma((4,)),
            dma((3,)), dma((4,)),
        ],
        compiler_params=pltpu.CompilerParams(
            collective_id=0, has_side_effects=True, vmem_limit_bytes=56 << 20
        ),
        name="parafac_half",
    )(
        slices, spectra.reshape(2 * rank, width), own_mix, held_mix,
        my_halves.astype(F32), system,
    )
    return (new_spectra, residual)


def solution(mesh):
    placed = (P("runs", None, "chan"), P(None, None, "chan"), P(), P(), P(), P())
    return jax.shard_map(
        functools.partial(body, mesh.shape["runs"]),
        mesh=mesh,
        in_specs=placed,
        out_specs=(P(None, None, "chan"), P("runs", None, "chan")),
        check_vma=False,
    )
```

```python
import functools

import jax
import jax.numpy as jnp
from jax import lax
from jax.experimental import pallas as pl
from jax.experimental.pallas import tpu as pltpu
from jax.sharding import PartitionSpec as P

NS_STEPS = 10
HI = lax.Precision.HIGHEST
F32 = jnp.float32
BF16 = jnp.bfloat16
NT = (((1,), (1,)), ((), ()))
MESH = pl.DeviceIdType.MESH


def mul(a, b):
    return jnp.dot(a, b, precision=HI, preferred_element_type=F32)


def identity(size):
    rows = lax.broadcasted_iota(jnp.int32, (size, size), 0)
    cols = lax.broadcasted_iota(jnp.int32, (size, size), 1)
    return (rows == cols).astype(F32)


def polar_rotate(mixes, bases):
    rank = mixes[0].shape[0]
    eye = identity(rank)
    scaled = [mul(m, b) for m, b in zip(mixes, bases)]
    grams = [lax.dot_general(s, s, NT, precision=HI, preferred_element_type=F32) for s in scaled]
    traces = [jnp.sum(jnp.sum(g * eye, axis=1, keepdims=True), axis=0, keepdims=True) + 1e-06 for g in grams]
    ys = [g / t for g, t in zip(grams, traces)]
    xs = [eye * lax.rsqrt(t) for t in traces]
    for step in range(NS_STEPS):
        zs = [1.5 * eye - 0.5 * y for y in ys]
        if step == 0:
            xs = [z * lax.rsqrt(t) for z, t in zip(zs, traces)]
        else:
            xs = [mul(x, z) for x, z in zip(xs, zs)]
        if step < NS_STEPS - 1:
            ws = [mul(y, z) for y, z in zip(ys, zs)]
            ys = [mul(w, z) for w, z in zip(ws, zs)]
    return [mul(x, s) for x, s in zip(xs, scaled)]


def invert_pair(systems):
    rank = systems[0].shape[0]
    eye = identity(rank)
    lane = lax.broadcasted_iota(jnp.int32, (rank, 2 * rank), 1)
    sub = lax.broadcasted_iota(jnp.int32, (rank, 2 * rank), 0)

    def step(j, tables):
        out = []
        for t in tables:
            col = jnp.sum(jnp.where(lane == j, t, 0.0), axis=1, keepdims=True)
            row = jnp.sum(jnp.where(sub == j, t, 0.0), axis=0, keepdims=True)
            pivot = jnp.sum(jnp.where(sub[:, :1] == j, col, 0.0), axis=0, keepdims=True)
            scaled = row / pivot
            out.append(jnp.where(sub == j, scaled, t - col * scaled))
        return out

    tables = [jnp.concatenate([a, eye], axis=1) for a in systems]
    tables = lax.fori_loop(0, rank, step, tables)
    return [t[:, rank:] for t in tables]


def kernel(
    n, sl, sp, omix, hmix, hf, halves, loadings, mixing, new_o, res_o,
    s, bs1, br1, own1, gb, psend, p32, rrecv, fitb, rows, gcat, bs2, br2, own2, rot,
    dsem, s1s, s1r, s2s, s2r, s3s, s3r, s4s, s4r, s5s, s5r, s6s, s6r,
):
    c = lax.axis_index("chan")
    r = lax.axis_index("runs")
    count, times, width = sl.shape
    rank = omix.shape[1]
    per = count // 4
    blocks = n // 2
    w = width // blocks
    peers = [(c + 2) % 4, 3 - c, c + 1 - 2 * (c % 2)]
    order = [p * per + i for p in peers + [c] for i in range(per)]

    def rows_of(k):
        return pl.ds(pl.multiple_of(k * times, times), times)

    loads = []
    for t, k in enumerate(order):
        load = pltpu.make_async_copy(sl.at[k], s.at[rows_of(k)], dsem.at[t])
        load.start()
        loads.append(load)

    barrier = pltpu.get_barrier_semaphore()
    for p in peers:
        pl.semaphore_signal(barrier, inc=1, device_id={"chan": p}, device_id_type=MESH)
    for d in range(1, n):
        pl.semaphore_signal(barrier, inc=1, device_id={"runs": (r + d) % n}, device_id_type=MESH)
    pl.semaphore_wait(barrier, 3 + n - 1)

    def remote(src, dst, ssem, rsem, where):
        return pltpu.make_async_remote_copy(
            src_ref=src, dst_ref=dst, send_sem=ssem, recv_sem=rsem, device_id=where, device_id_type=MESH
        )

    def basis_phase(both, flip, bs, br, own, ssem, rsem, waits):
        sends = []
        for t, k in enumerate(order):
            if waits:
                loads[t].wait()
            part = lax.dot_general(s[rows_of(k)], both, NT, preferred_element_type=F32).T
            h = hf[k]
            if flip:
                h = 1.0 - h
            chosen = part[:rank] * (1.0 - h) + part[rank:] * h
            q, i = t // per, t % per
            if q < 3:
                bs[k] = chosen
                if i == per - 1:
                    p = peers[q]
                    send = remote(
                        bs.at[pl.ds(p * per, per)], br.at[c], ssem.at[q], rsem.at[c], {"chan": p}
                    )
                    send.start()
                    sends.append(send)
            else:
                own[i] = chosen
        return sends

    def basis_sum(bs, br, own, ssem, rsem):
        for q, p in enumerate(peers):
            remote(
                bs.at[pl.ds(p * per, per)], br.at[p], ssem.at[q], rsem.at[p], {"chan": p}
            ).wait_recv()
        return [
            own[i] + br[peers[0], i] + br[peers[1], i] + br[peers[2], i]
            for i in range(per)
        ]

    def share(buf, ssem, rsem):
        mine = buf.at[pl.ds(c * per, per)]
        sends = []
        for q, p in enumerate(peers):
            send = remote(mine, mine, ssem.at[q], rsem.at[c], {"chan": p})
            send.start()
            sends.append(send)
        return sends

    def shared(buf, ssem, rsem):
        for q, p in enumerate(peers):
            theirs = buf.at[pl.ds(p * per, per)]
            remote(theirs, theirs, ssem.at[q], rsem.at[p], {"chan": p}).wait_recv()

    sends = basis_phase(sp[...], False, bs1, br1, own1, s1s, s1r, True)
    second = halves[...].astype(F32)
    every = loadings[...]
    systems = []
    for half, member in enumerate((1.0 - second, second)):
        part = (every * member).T
        mix = mixing[half]
        systems.append(mul(mix.T, mix) * mul(part, every))
    inverses = invert_pair(systems)
    backs = []
    for i in range(per):
        h = hf[c * per + i]
        chosen = inverses[0] * (1.0 - h) + inverses[1] * h
        backs.append(
            lax.dot_general(chosen, omix[c * per + i], NT, precision=HI, preferred_element_type=F32)
        )
    bases = basis_sum(bs1, br1, own1, s1s, s1r)
    rotated = polar_rotate([omix[c * per + i] for i in range(per)], bases)
    for i in range(per):
        low = rotated[i].astype(BF16).astype(F32)
        gb[c * per + i] = mul(backs[i], low).astype(BF16)
    sends += share(gb, s2s, s2r)
    shared(gb, s2s, s2r)
    for k in range(count):
        h = hf[k]
        g = gb[k].astype(F32)
        gcat[:rank, k * times : (k + 1) * times] = (g * (1.0 - h)).astype(BF16)
        gcat[rank:, k * times : (k + 1) * times] = (g * h).astype(BF16)

    def chunk(block):
        cols = pl.ds(pl.multiple_of(block * w, w), w)
        return jnp.dot(gcat[...], s[:, cols], preferred_element_type=F32)

    def send_chunk(j, d):
        send = remote(psend.at[j], rrecv.at[r], s3s.at[d], s3r.at[r], {"runs": j})
        send.start()
        sends.append(send)

    count_sent = 0
    for step in range(1, blocks):
        block = (r + step) % blocks
        part = chunk(block)
        for half in range(2):
            j = half * blocks + block
            psend[j] = part[half * rank : (half + 1) * rank].astype(BF16)
            send_chunk(j, count_sent)
            count_sent += 1
    part = chunk(r % blocks)
    p32[0] = part[:rank]
    p32[1] = part[rank:]
    j = (r + blocks) % n
    psend[j] = p32[1 - r // blocks].astype(BF16)
    send_chunk(j, count_sent)
    total = p32[r // blocks]
    for d in range(1, n):
        j = (r + d) % n
        remote(psend.at[j], rrecv.at[j], s3s.at[d - 1], s3r.at[j], {"runs": j}).wait_recv()
        total = total + rrecv[j].astype(F32)
    fitb[r] = total.astype(BF16)
    for d in range(1, n):
        send = remote(fitb.at[r], fitb.at[r], s4s.at[d - 1], s4r.at[r], {"runs": (r + d) % n})
        send.start()
        sends.append(send)
    for d in range(1, n):
        j = (r + d) % n
        remote(fitb.at[j], fitb.at[j], s4s.at[d - 1], s4r.at[j], {"runs": j}).wait_recv()
    for half in range(2):
        for block in range(blocks):
            low = fitb[half * blocks + block]
            rows[half * rank : (half + 1) * rank, block * w : (block + 1) * w] = low
            new_o[half, :, block * w : (block + 1) * w] = low

    sends += basis_phase(rows[...], True, bs2, br2, own2, s5s, s5r, False)

    def model(k):
        h = hf[k]
        m = hmix[k]
        high = m.astype(BF16).astype(F32)
        parts = [high, m - high]
        left = jnp.concatenate(
            [jnp.concatenate([v * h, v * (1.0 - h)], axis=1) for v in parts], axis=0
        ).astype(BF16)
        both = jnp.dot(left, rows[...], preferred_element_type=F32)
        return both[:rank] + both[rank:]

    for k in range(count):
        res_o[k] = model(k)
    bases = basis_sum(bs2, br2, own2, s5s, s5r)
    rotated = polar_rotate([hmix[c * per + i] for i in range(per)], bases)
    for i in range(per):
        rot[c * per + i] = rotated[i].astype(BF16)
    sends += share(rot, s6s, s6r)
    shared(rot, s6s, s6r)
    for k in range(count):
        res_o[k] = (
            jnp.dot(rot[k], s[k * times : (k + 1) * times], preferred_element_type=F32) - res_o[k]
        )
    for send in sends:
        send.wait_send()


def body(n, slices, spectra, loadings, mixing, halves, partner):
    run_count, times, width = slices.shape
    rank = mixing.shape[-1]
    total_runs = loadings.shape[0]
    first_run = lax.axis_index("runs") * run_count
    mine = first_run + jnp.arange(run_count, dtype=jnp.int32)
    all_runs = jnp.arange(total_runs, dtype=jnp.int32)
    matches = all_runs[None, :] == mine[:, None]
    my_halves = jnp.sum(jnp.where(matches, halves[None, :], 0), axis=1)
    my_mates = jnp.sum(jnp.where(matches, partner[None, :], 0), axis=1)
    my_loads = jnp.dot(matches.astype(F32), loadings, precision=HI)
    mate_match = (all_runs[None, :] == my_mates[:, None]).astype(F32)
    mate_loads = jnp.dot(mate_match, loadings, precision=HI)
    first_half = (my_halves == 0)[:, None, None]
    own_mix = jnp.where(first_half, mixing[0][None], mixing[1][None]) * my_loads[:, None, :]
    held_mix = jnp.where(first_half, mixing[1][None], mixing[0][None]) * mate_loads[:, None, :]

    per = run_count // 4
    w = 2 * width // n
    vmem = pl.BlockSpec(memory_space=pltpu.VMEM)
    dma = pltpu.SemaphoreType.DMA
    new_spectra, residual = pl.pallas_call(
        functools.partial(kernel, n),
        out_shape=(
            jax.ShapeDtypeStruct((2, rank, width), BF16),
            jax.ShapeDtypeStruct((run_count, rank, width), F32),
        ),
        in_specs=[
            pl.BlockSpec(memory_space=pl.ANY), vmem, vmem, vmem,
            pl.BlockSpec(memory_space=pltpu.SMEM), vmem, vmem, vmem,
        ],
        out_specs=(vmem, vmem),
        scratch_shapes=[
            pltpu.VMEM((run_count * times, width), BF16),
            pltpu.VMEM((run_count, rank, times), F32),
            pltpu.VMEM((4, per, rank, times), F32),
            pltpu.VMEM((per, rank, times), F32),
            pltpu.VMEM((run_count, rank, times), BF16),
            pltpu.VMEM((n, rank, w), BF16),
            pltpu.VMEM((2, rank, w), F32),
            pltpu.VMEM((n, rank, w), BF16),
            pltpu.VMEM((n, rank, w), BF16),
            pltpu.VMEM((2 * rank, width), BF16),
            pltpu.VMEM((2 * rank, run_count * times), BF16),
            pltpu.VMEM((run_count, rank, times), F32),
            pltpu.VMEM((4, per, rank, times), F32),
            pltpu.VMEM((per, rank, times), F32),
            pltpu.VMEM((run_count, rank, times), BF16),
            dma((run_count,)),
            dma((3,)), dma((4,)),
            dma((3,)), dma((4,)),
            dma((n - 1,)), dma((n,)),
            dma((n - 1,)), dma((n,)),
            dma((3,)), dma((4,)),
            dma((3,)), dma((4,)),
        ],
        compiler_params=pltpu.CompilerParams(
            collective_id=0, has_side_effects=True, vmem_limit_bytes=56 << 20
        ),
        name="parafac_half",
    )(
        slices, spectra.reshape(2 * rank, width), own_mix, held_mix,
        my_halves.astype(F32), halves[:, None], loadings, mixing,
    )
    return (new_spectra.astype(F32), residual)


def solution(mesh):
    placed = (P("runs", None, "chan"), P(None, None, "chan"), P(), P(), P(), P())
    return jax.shard_map(
        functools.partial(body, mesh.shape["runs"]),
        mesh=mesh,
        in_specs=placed,
        out_specs=(P(None, None, "chan"), P("runs", None, "chan")),
        check_vma=False,
    )
```
